32 devices in a mesh: row: 8 (over z, y), col: 4 (over x, core).
Axes of the slice: x: 2, y: 2, z: 4, core: 2. Of those that a mesh axis runs over, the one named last changes fastest.
Arguments:
- queries: bfloat16 [4096, 768], P(('row', 'col')), may hold values from -6 to 6
- key_rows: bfloat16 [4096, 768], P(('col', 'row')), may hold values from -6 to 6
- values: bfloat16 [4096, 768], P(('col', 'row')), may hold values from -6 to 6
- out_grad: bfloat16 [4096, 768], P(('row', 'col')), may hold values from -6 to 6
- block_pairs: int32 [32, 32, 2], P(('row', 'col')), may hold values from 0 to 7, as said below
- pair_count: int32 [32], P(('row', 'col')), may hold values from 1 to 32, as said below
- edge_mask: int32 [32, 32, 128, 128], P(('row', 'col')), may hold values from 0 to 1, as said below
Outputs:
- attention_out: bfloat16 [4096, 768], P(('row', 'col'))
- query_grad: float32 [4096, 768], P(('row', 'col'))
- key_grad: float32 [4096, 768], P(('col', 'row'))
- value_grad: float32 [4096, 768], P(('col', 'row'))
The draws below stay inside these ranges and needn't reach their ends.
Inputs may be any that keep to these rules, and one draw needn't show every extreme that they name: `block_pairs`: the slots of one device name distinct block pairs of its tile, the first coordinate below 4, the second below 8. Every block pair of a target block with the source block of the same global number stands among the live slots of its device. `pair_count`: some device has all 32 slots live. `edge_mask`: in every live block pair of a target block with the source block of the same number, each node has an edge to itself and to the node whose index differs in the lowest bit.
All inputs are finite; a program needn't handle non-finite values.
Results may differ from the reference program's by a relative error of at most 0.015.
Values may be sent and summed in bfloat16 or wider, within the bound.
A program may use at most 192 MiB of HBM per device.

```python
import jax
import jax.numpy as jnp
from jax import lax

HEADS = 8
HEAD_DIM = 96
WIDTH = 768
BLOCK = 128
NODES = 4096
TGT_BLOCKS = 4
SRC_BLOCKS = 8
SLOTS = 32
N_ROW = 8
N_COL = 4


def tile_layout():
    device_count = N_ROW * N_COL
    tile_size = TGT_BLOCKS * SRC_BLOCKS
    device_ids = jnp.arange(device_count, dtype=jnp.int32)[:, None]
    cells = jnp.arange(tile_size, dtype=jnp.int32)[None, :]
    target_local = jnp.broadcast_to(cells // SRC_BLOCKS, (device_count, tile_size))
    source_local = jnp.broadcast_to(cells % SRC_BLOCKS, (device_count, tile_size))
    target_global = device_ids // N_COL * TGT_BLOCKS + target_local
    source_global = device_ids % N_COL * SRC_BLOCKS + source_local
    return (target_local, source_local, target_global == source_global)


def pair_layout(key):
    target_local, source_local, diagonal = tile_layout()
    device_count = N_ROW * N_COL
    tile_size = TGT_BLOCKS * SRC_BLOCKS
    ranks = jax.vmap(lambda subkey: jax.random.permutation(subkey, tile_size))(jax.random.split(key, device_count))
    priority = jnp.where(diagonal, 0, tile_size) + ranks.astype(jnp.int32)
    order = jnp.argsort(priority, axis=1)[:, :SLOTS]
    target_pick = jnp.take_along_axis(target_local, order, axis=1)
    source_pick = jnp.take_along_axis(source_local, order, axis=1)
    diagonal_pick = jnp.take_along_axis(diagonal, order, axis=1)
    pairs = jnp.stack([target_pick, source_pick], axis=-1).astype(jnp.int32)
    return (pairs, diagonal_pick)


def draw_block_pairs(key, part):
    pairs, diagonal_pick = pair_layout(key)
    return pairs


def draw_pair_count(key, part):
    key = jax.random.fold_in(key, 11)
    first_key, second_key = jax.random.split(key)
    device_count = N_ROW * N_COL
    target_local, source_local, diagonal = tile_layout()
    diagonal_count = jnp.sum(diagonal.astype(jnp.int32), axis=1)
    base = jax.random.randint(first_key, (device_count,), max(1, SLOTS // 2), SLOTS + 1)
    full_count = max(1, device_count // 4)
    placing = jax.random.permutation(second_key, device_count)
    counts = jnp.where(placing < full_count, SLOTS, jnp.maximum(base, diagonal_count))
    return counts.astype(jnp.int32)


def draw_edge_mask(key, part):
    pairs, diagonal_pick = pair_layout(key)
    key = jax.random.fold_in(key, 13)
    device_count = N_ROW * N_COL
    random_edges = jax.random.randint(key, (device_count, SLOTS, BLOCK, BLOCK), 0, 8) == 0
    row_ids = jnp.arange(BLOCK, dtype=jnp.int32)[:, None]
    column_ids = jnp.arange(BLOCK, dtype=jnp.int32)[None, :]
    forced = (row_ids == column_ids) | (column_ids == jnp.bitwise_xor(row_ids, 1))
    edges = random_edges | diagonal_pick[:, :, None, None] & forced[None, None, :, :]
    return edges.astype(jnp.int32)


def draw_queries(key, part):
    key = jax.random.fold_in(key, 3)
    return jnp.clip(jax.random.normal(key, (NODES, WIDTH), jnp.float32), -6.0, 6.0).astype(jnp.bfloat16)


def draw_key_rows(key, part):
    key = jax.random.fold_in(key, 5)
    return jnp.clip(jax.random.normal(key, (NODES, WIDTH), jnp.float32), -6.0, 6.0).astype(jnp.bfloat16)


def steps_of(own_key, extent, shards, least, largest):
    factor_of, own = 1.0, jax.random.fold_in(own_key, 6)
    for axis_at, parts in shards:
        heights = jnp.exp(jax.random.uniform(jax.random.fold_in(own, axis_at), (parts,), jnp.float32, least / len(shards), largest / len(shards)))
        factor_of = factor_of * jnp.repeat(heights, extent[axis_at] // parts).reshape([-1 if axis == axis_at else 1 for axis in range(len(extent))])
    return factor_of


def normal_values(key, shape, spread, reach, cuts=(), kind=jnp.bfloat16):
    result = spread * jax.random.normal(key, shape, jnp.float32)
    if cuts:
        result = result * steps_of(key, shape, cuts, -0.22, 0.18)
    return jnp.clip(result, -reach, reach).astype(kind)


def setup_inputs(seed: int = 0) -> dict:
    seeds = jax.random.split(jax.random.key(seed), 8)
    queries = draw_queries(jax.random.fold_in(seeds[7], 71), 0)
    key_rows = draw_key_rows(jax.random.fold_in(seeds[7], 71), 0)
    values = normal_values(seeds[2], (NODES, WIDTH), 1.0, 6.0, ((0, 32),))
    out_grad = normal_values(seeds[3], (NODES, WIDTH), 1.0, 6.0, ((0, 32),))
    block_pairs = draw_block_pairs(jax.random.fold_in(seeds[7], 71), 0)
    pair_count = draw_pair_count(jax.random.fold_in(seeds[7], 71), 0)
    edge_mask = draw_edge_mask(jax.random.fold_in(seeds[7], 71), 0)
    return {"queries": queries, "key_rows": key_rows, "values": values, "out_grad": out_grad, "block_pairs": block_pairs, "pair_count": pair_count, "edge_mask": edge_mask}


NEGATIVE = -1.0e30


def reference(queries, key_rows, values, out_grad, block_pairs, pair_count, edge_mask):
    score_scale = HEAD_DIM ** -0.5
    highest = lax.Precision.HIGHEST
    device_count = N_ROW * N_COL
    total_slots = device_count * SLOTS
    block_count = NODES // BLOCK
    flat_slots = jnp.arange(total_slots, dtype=jnp.int32)
    device_ids = flat_slots // SLOTS
    slot_ids = flat_slots % SLOTS
    live_slots = slot_ids < pair_count[device_ids]
    target_ids = ((device_ids // N_COL) * TGT_BLOCKS + block_pairs[device_ids, slot_ids, 0]).astype(jnp.int32)
    source_ids = ((device_ids % N_COL) * SRC_BLOCKS + block_pairs[device_ids, slot_ids, 1]).astype(jnp.int32)
    mask_tiles = edge_mask.reshape(total_slots, BLOCK, BLOCK)
    query_blocks = queries.astype(jnp.float32).reshape(block_count, BLOCK, HEADS, HEAD_DIM)
    key_blocks = key_rows.astype(jnp.float32).reshape(block_count, BLOCK, HEADS, HEAD_DIM)
    value_blocks = values.astype(jnp.float32).reshape(block_count, BLOCK, HEADS, HEAD_DIM)
    grad_blocks = out_grad.astype(jnp.float32).reshape(block_count, BLOCK, HEADS, HEAD_DIM)
    slot_items = (target_ids, source_ids, live_slots, mask_tiles)

    def scores_of(target, source, mask_tile):
        scores = jnp.einsum("ihd,jhd->hij", query_blocks[target], key_blocks[source], precision=highest) * score_scale
        return scores, (mask_tile > 0)[None, :, :]

    def max_step(running, slot_item):
        target, source, is_live, mask_tile = slot_item

        def update(current):
            scores, keep_mask = scores_of(target, source, mask_tile)
            row_top = jnp.max(jnp.where(keep_mask, scores, NEGATIVE), axis=2)
            return current.at[target].max(row_top)

        return lax.cond(is_live, update, lambda current: current, running), None

    row_max = lax.scan(max_step, jnp.full((block_count, HEADS, BLOCK), NEGATIVE, jnp.float32), slot_items)[0]

    def sum_step(carry, slot_item):
        target, source, is_live, mask_tile = slot_item

        def update(current):
            numer_sum, weight_sum = current
            scores, keep_mask = scores_of(target, source, mask_tile)
            weights = jnp.exp(jnp.where(keep_mask, scores - row_max[target][:, :, None], NEGATIVE))
            rounded = lax.optimization_barrier(weights.astype(jnp.bfloat16)).astype(jnp.float32)
            mixed = jnp.einsum("hij,jhd->ihd", rounded, value_blocks[source], precision=highest)
            return numer_sum.at[target].add(mixed), weight_sum.at[target].add(jnp.sum(weights, axis=2))

        return lax.cond(is_live, update, lambda current: current, carry), None

    numer_init = jnp.zeros((block_count, BLOCK, HEADS, HEAD_DIM), jnp.float32)
    total_init = jnp.zeros((block_count, HEADS, BLOCK), jnp.float32)
    numer_sum, row_total = lax.scan(sum_step, (numer_init, total_init), slot_items)[0]
    heads_out = numer_sum / jnp.transpose(row_total, (0, 2, 1))[..., None]
    attention_out = heads_out.astype(jnp.bfloat16).reshape(NODES, WIDTH)
    products = grad_blocks * attention_out.astype(jnp.float32).reshape(block_count, BLOCK, HEADS, HEAD_DIM)
    row_delta = jnp.transpose(jnp.sum(products, axis=3), (0, 2, 1))

    def back_step(carry, slot_item):
        target, source, is_live, mask_tile = slot_item

        def update(current):
            query_acc, key_acc, value_acc = current
            scores, keep_mask = scores_of(target, source, mask_tile)
            probs = jnp.exp(jnp.where(keep_mask, scores - row_max[target][:, :, None], NEGATIVE)) / row_total[target][:, :, None]
            grad_dots = jnp.einsum("ihd,jhd->hij", grad_blocks[target], value_blocks[source], precision=highest)
            score_grads = probs * (grad_dots - row_delta[target][:, :, None]) * score_scale
            score_grads = lax.optimization_barrier(score_grads.astype(jnp.bfloat16)).astype(jnp.float32)
            probs_rounded = lax.optimization_barrier(probs.astype(jnp.bfloat16)).astype(jnp.float32)
            query_acc = query_acc.at[target].add(jnp.einsum("hij,jhd->ihd", score_grads, key_blocks[source], precision=highest))
            key_acc = key_acc.at[source].add(jnp.einsum("hij,ihd->jhd", score_grads, query_blocks[target], precision=highest))
            value_acc = value_acc.at[source].add(jnp.einsum("hij,ihd->jhd", probs_rounded, grad_blocks[target], precision=highest))
            return query_acc, key_acc, value_acc

        return lax.cond(is_live, update, lambda current: current, carry), None

    grad_init = jnp.zeros((block_count, BLOCK, HEADS, HEAD_DIM), jnp.float32)
    query_acc, key_acc, value_acc = lax.scan(back_step, (grad_init, grad_init, grad_init), slot_items)[0]
    return (attention_out, query_acc.reshape(NODES, WIDTH), key_acc.reshape(NODES, WIDTH), value_acc.reshape(NODES, WIDTH))
```

```python
import functools

import jax
import jax.numpy as jnp
from jax import lax
from jax.experimental import pallas as pl
from jax.experimental.pallas import tpu as pltpu
from jax.sharding import PartitionSpec as P

HEADS = 8
HEAD_DIM = 96
BLOCK = 128


NEGATIVE = -1e30


def on_device(queries, key_rows, values, out_grad, block_pairs, pair_count, edge_mask):
    score_scale = HEAD_DIM ** (-0.5)
    targets, cotangent = (
        lax.all_gather(queries, "col", axis=0, tiled=True),
        lax.all_gather(out_grad, "col", axis=0, tiled=True),
    )
    sources, source_values = (
        lax.all_gather(key_rows, "row", axis=0, tiled=True),
        lax.all_gather(values, "row", axis=0, tiled=True),
    )
    own_rows = queries.shape[0]
    target_rows = targets.shape[0]
    source_rows = sources.shape[0]
    target_blocks = target_rows // BLOCK
    source_blocks = source_rows // BLOCK
    query_blocks = targets.reshape(target_blocks, BLOCK, HEADS, HEAD_DIM)
    grad_blocks = cotangent.reshape(target_blocks, BLOCK, HEADS, HEAD_DIM)
    key_blocks = sources.reshape(source_blocks, BLOCK, HEADS, HEAD_DIM)
    value_blocks = source_values.reshape(source_blocks, BLOCK, HEADS, HEAD_DIM)
    slot_total = edge_mask.shape[1]
    group_size = min(8, slot_total)
    turn_count = slot_total // group_size
    pair_list = block_pairs[0]
    live_slots = jnp.arange(slot_total, dtype=jnp.int32) < pair_count[0]
    keep_all = (edge_mask[0] > 0) & live_slots[:, None, None]

    def group_scores(turn_index):
        first_slot = turn_index * group_size
        target_ids = lax.dynamic_slice_in_dim(pair_list[:, 0], first_slot, group_size)
        source_ids = lax.dynamic_slice_in_dim(pair_list[:, 1], first_slot, group_size)
        keep_mask = lax.dynamic_slice_in_dim(keep_all, first_slot, group_size, 0)[:, None, :, :]
        scores = (
            jnp.einsum(
                "gihd,gjhd->ghij",
                query_blocks[target_ids],
                key_blocks[source_ids],
                preferred_element_type=jnp.float32,
            )
            * score_scale
        )
        return (target_ids, source_ids, keep_mask, scores)

    def max_turn(turn_index, running_max):
        target_ids, source_ids, keep_mask, scores = group_scores(turn_index)
        row_top = jnp.max(jnp.where(keep_mask, scores, NEGATIVE), axis=3)
        return running_max.at[target_ids].max(row_top)

    local_max = lax.fori_loop(
        0, turn_count, max_turn, jnp.full((target_blocks, HEADS, BLOCK), NEGATIVE, jnp.float32)
    )
    row_max = lax.pmax(local_max, "col")

    def sum_turn(turn_index, carry):
        numer_sum, weight_sum = carry
        target_ids, source_ids, keep_mask, scores = group_scores(turn_index)
        weights = jnp.exp(jnp.where(keep_mask, scores - row_max[target_ids][..., None], NEGATIVE))
        rounded = weights.astype(jnp.bfloat16)
        mixed = jnp.einsum(
            "ghij,gjhd->gihd", rounded, value_blocks[source_ids], preferred_element_type=jnp.float32
        )
        numer_sum = numer_sum.at[target_ids].add(mixed.reshape(group_size, BLOCK, HEADS * HEAD_DIM))
        weight_sum = weight_sum.at[target_ids].add(jnp.sum(weights, axis=3))
        return (numer_sum, weight_sum)

    numer_init = jnp.zeros((target_blocks, BLOCK, HEADS * HEAD_DIM), jnp.float32)
    total_init = jnp.zeros((target_blocks, HEADS, BLOCK), jnp.float32)
    numer_sum, weight_sum = lax.fori_loop(0, turn_count, sum_turn, (numer_init, total_init))
    numer_flat = numer_sum.reshape(target_rows, HEADS * HEAD_DIM)
    numer_all, total_all = lax.psum((numer_flat, weight_sum), "col")
    heads_out = (
        numer_all.reshape(target_blocks, BLOCK, HEADS, HEAD_DIM)
        / jnp.transpose(total_all, (0, 2, 1))[..., None]
    )
    out_all = heads_out.astype(jnp.bfloat16).reshape(target_rows, HEADS * HEAD_DIM)
    attention_out = lax.dynamic_slice_in_dim(out_all, lax.axis_index("col") * own_rows, own_rows, 0)
    products = (cotangent.astype(jnp.float32) * out_all.astype(jnp.float32)).reshape(
        target_blocks, BLOCK, HEADS, HEAD_DIM
    )
    row_delta = jnp.transpose(jnp.sum(products, axis=3), (0, 2, 1))

    def back_turn(turn_index, carry):
        query_acc, key_acc, value_acc = carry
        target_ids, source_ids, keep_mask, scores = group_scores(turn_index)
        probs = (
            jnp.exp(jnp.where(keep_mask, scores - row_max[target_ids][..., None], NEGATIVE))
            / total_all[target_ids][..., None]
        )
        grad_group = grad_blocks[target_ids]
        grad_dots = jnp.einsum(
            "gihd,gjhd->ghij",
            grad_group,
            value_blocks[source_ids],
            preferred_element_type=jnp.float32,
        )
        score_grads = (probs * (grad_dots - row_delta[target_ids][..., None]) * score_scale).astype(
            jnp.bfloat16
        )
        probs_rounded = probs.astype(jnp.bfloat16)
        query_part = jnp.einsum(
            "ghij,gjhd->gihd",
            score_grads,
            key_blocks[source_ids],
            preferred_element_type=jnp.float32,
        )
        key_part = jnp.einsum(
            "ghij,gihd->gjhd",
            score_grads,
            query_blocks[target_ids],
            preferred_element_type=jnp.float32,
        )
        value_part = jnp.einsum(
            "ghij,gihd->gjhd", probs_rounded, grad_group, preferred_element_type=jnp.float32
        )
        query_acc = query_acc.at[target_ids].add(
            query_part.reshape(group_size, BLOCK, HEADS * HEAD_DIM)
        )
        key_acc = key_acc.at[source_ids].add(key_part.reshape(group_size, BLOCK, HEADS * HEAD_DIM))
        value_acc = value_acc.at[source_ids].add(
            value_part.reshape(group_size, BLOCK, HEADS * HEAD_DIM)
        )
        return (query_acc, key_acc, value_acc)

    query_init = jnp.zeros((target_blocks, BLOCK, HEADS * HEAD_DIM), jnp.float32)
    source_init = jnp.zeros((source_blocks, BLOCK, HEADS * HEAD_DIM), jnp.float32)
    query_acc, key_acc, value_acc = lax.fori_loop(
        0, turn_count, back_turn, (query_init, source_init, source_init)
    )
    query_grad = lax.psum_scatter(
        query_acc.reshape(target_rows, HEADS * HEAD_DIM), "col", scatter_dimension=0, tiled=True
    )
    key_grad, value_grad = (
        lax.psum_scatter(
            key_acc.reshape(source_rows, HEADS * HEAD_DIM), "row", scatter_dimension=0, tiled=True
        ),
        lax.psum_scatter(
            value_acc.reshape(source_rows, HEADS * HEAD_DIM), "row", scatter_dimension=0, tiled=True
        ),
    )
    return (attention_out, query_grad, key_grad, value_grad)


MASKED = -1e30
FLOOR = -1e28
MESH = pl.DeviceIdType.MESH


def contract(left, right, left_dim, right_dim):
    return lax.dot_general(
        left,
        right,
        (((left_dim,), (right_dim,)), ((), ())),
        preferred_element_type=jnp.float32,
    )


def prepare_kernel(pair_ref, count_ref, q_ref, k_ref, v_ref, g_ref, mask_ref, qg_ref, kv_ref, bias_ref):
    for src, dst, first in ((q_ref, qg_ref, 0), (g_ref, qg_ref, HEADS), (k_ref, kv_ref, 0), (v_ref, kv_ref, HEADS)):
        turned = jnp.transpose(src[...].astype(jnp.float32)).astype(jnp.bfloat16)
        dst[first : first + HEADS] = turned.reshape(HEADS, HEAD_DIM, BLOCK)
    bias_ref[...] = jnp.full(bias_ref.shape, MASKED, jnp.float32)

    @pl.loop(0, count_ref[0])
    def _(slot):
        target = pair_ref[slot, 0]
        source = pair_ref[slot, 1]
        kept = jnp.transpose(mask_ref[slot].astype(jnp.float32))
        bias_ref[source, target] = jnp.where(kept > 0.5, 0.0, MASKED)


def layer_kernel(
    n_ring,
    qg_own,
    kv_own,
    bias_ref,
    att_ref,
    qgrad_ref,
    kgrad_ref,
    vgrad_ref,
    kv_buf,
    qg_buf,
    weight_buf,
    dots_buf,
    chunk_stats,
    stat_buf,
    factor_buf,
    delta_buf,
    acc_buf,
    part_buf,
    right_out,
    right_in,
    left_out,
    left_in,
    core_out,
    core_in,
    chip_out,
    chip_in,
    ring_send,
    ring_recv,
    qg_send,
    qg_recv,
    stat_send,
    stat_recv,
    sum_send,
    sum_recv,
    col_send,
    col_recv,
    own_sem,
):
    scale = HEAD_DIM ** (-0.5)
    row = lax.axis_index("row")
    col = lax.axis_index("col")
    half_ring = n_ring // 2
    depth, side = row // 2, row % 2
    place = jnp.where(side == 0, depth, n_ring - 1 - depth)

    def row_at(position):
        wrapped = lax.rem(position + 2 * n_ring, n_ring)
        return jnp.where(wrapped < half_ring, 2 * wrapped, 2 * (n_ring - 1 - wrapped) + 1)

    right = (row_at(place + 1), col)
    left = (row_at(place - 1), col)
    core_col = col + 1 - 2 * (col % 2)
    chip_col = (col + 2) % 4
    core_peer = (row, core_col)
    chip_peer = (row, chip_col)
    others = [(row, (col + k) % 4) for k in range(1, 4)]
    pending = []

    def send(src, dst, send_sem, recv_sem, device):
        copy = pltpu.make_async_remote_copy(
            src_ref=src,
            dst_ref=dst,
            send_sem=send_sem,
            recv_sem=recv_sem,
            device_id=device,
            device_id_type=MESH,
        )
        copy.start()
        pending.append(copy)
        return copy

    barrier = pltpu.get_barrier_semaphore()
    for device in [right, left] + others:
        pl.semaphore_signal(barrier, inc=1, device_id=device, device_id_type=MESH)
    pl.semaphore_wait(barrier, 5)

    def lanes(index):
        return pl.ds(pl.multiple_of(index * BLOCK, BLOCK), BLOCK)

    def ring_right(step):
        part = pl.ds(0, 2 * HEADS if step < half_ring else HEADS)
        src = kv_own if step == 1 else kv_buf.at[step - 1]
        return send(
            src.at[part], kv_buf.at[step, part], ring_send.at[step], ring_recv.at[step], right
        )

    def ring_left(step):
        part = pl.ds(0, 2 * HEADS) if step < half_ring else pl.ds(HEADS, HEADS)
        src = kv_own if step == 1 else kv_buf.at[n_ring - step + 1]
        return send(
            src.at[part],
            kv_buf.at[n_ring - step, part],
            ring_send.at[half_ring + step],
            ring_recv.at[half_ring + step],
            left,
        )

    from_chip = send(qg_own, qg_buf.at[:, :, lanes(col)], qg_send.at[0], qg_recv.at[0], chip_peer)
    from_core = send(qg_own, qg_buf.at[:, :, lanes(col)], qg_send.at[1], qg_recv.at[1], core_peer)
    on_right = ring_right(1)
    on_left = ring_left(1)
    own_copy = pltpu.make_async_copy(qg_own, qg_buf.at[:, :, lanes(col)], own_sem.at[0])
    own_copy.start()
    kv_buf[0] = kv_own[...]
    own_copy.wait()
    from_chip.wait_recv()
    passed = send(
        qg_buf.at[:, :, lanes(chip_col)],
        qg_buf.at[:, :, lanes(chip_col)],
        qg_send.at[2],
        qg_recv.at[2],
        core_peer,
    )
    from_core.wait_recv()
    passed.wait_recv()

    width = 2 * BLOCK
    parts = qg_buf.shape[2] // width

    def stats_of(slot):
        source = row_at(place - slot)

        @pl.loop(0, HEADS)
        def _(head):
            key_t = kv_buf[slot, head]
            value_t = kv_buf[slot, HEADS + head]
            for part in range(parts):
                cut = pl.ds(part * width, width)
                bias = jnp.concatenate(
                    [bias_ref[source, 2 * part], bias_ref[source, 2 * part + 1]], axis=1
                )
                scores = contract(key_t, qg_buf[head, :, cut], 0, 0) * scale + bias
                dots = contract(value_t, qg_buf[HEADS + head, :, cut], 0, 0)
                top = jnp.maximum(jnp.max(scores, axis=0, keepdims=True), FLOOR)
                weights = jnp.exp(scores - top)
                weight_buf[slot, head, :, cut] = weights
                dots_buf[slot, head, :, cut] = dots
                chunk_stats[slot, head, 0:1, cut] = top
                chunk_stats[slot, head, 1:2, cut] = jnp.sum(weights, axis=0, keepdims=True)
                chunk_stats[slot, head, 2:3, cut] = jnp.sum(weights * dots, axis=0, keepdims=True)

    stats_of(0)
    for step in range(1, half_ring + 1):
        on_right.wait_recv()
        last_right = on_right
        if step < half_ring:
            on_right = ring_right(step + 1)
        on_left.wait_recv()
        if step < half_ring:
            on_left = ring_left(step + 1)
            stats_of(step)
            stats_of(n_ring - step)
        else:
            stats_of(step)

    @pl.loop(0, HEADS)
    def _(head):
        top = chunk_stats[0, head, 0:1]
        for slot in range(1, n_ring):
            top = jnp.maximum(top, chunk_stats[slot, head, 0:1])
        total = jnp.zeros_like(top)
        mixed = jnp.zeros_like(top)
        for slot in range(n_ring):
            factor = jnp.exp(chunk_stats[slot, head, 0:1] - top)
            total = total + factor * chunk_stats[slot, head, 1:2]
            mixed = mixed + factor * chunk_stats[slot, head, 2:3]
        stat_buf[0, head, 0:1] = top
        stat_buf[0, head, 1:2] = total
        stat_buf[0, head, 2:3] = mixed

    shared = [
        send(stat_buf.at[0], stat_buf.at[k], stat_send.at[k], stat_recv.at[k], others[k - 1])
        for k in range(1, 4)
    ]
    acc_buf[...] = jnp.zeros(acc_buf.shape, jnp.float32)
    for copy in shared:
        copy.wait_recv()

    @pl.loop(0, HEADS)
    def _(head):
        top = stat_buf[0, head, 0:1]
        for k in range(1, 4):
            top = jnp.maximum(top, stat_buf[k, head, 0:1])
        total = jnp.zeros_like(top)
        mixed = jnp.zeros_like(top)
        for k in range(4):
            factor = jnp.exp(stat_buf[k, head, 0:1] - top)
            total = total + factor * stat_buf[k, head, 1:2]
            mixed = mixed + factor * stat_buf[k, head, 2:3]
        inverse = 1.0 / total
        delta_buf[head, 0:1] = mixed * inverse
        for slot in range(n_ring):
            factor_buf[head, slot : slot + 1] = (
                jnp.exp(chunk_stats[slot, head, 0:1] - top) * inverse
            )

    def grads_of(slot):
        @pl.loop(0, HEADS)
        def _(head):
            key_t = kv_buf[slot, head]
            value_t = kv_buf[slot, HEADS + head]
            key_part = jnp.zeros((HEAD_DIM, BLOCK), jnp.float32)
            value_part = jnp.zeros((HEAD_DIM, BLOCK), jnp.float32)
            for part in range(parts):
                cut = pl.ds(part * width, width)
                probs = weight_buf[slot, head, :, cut] * factor_buf[head, slot : slot + 1, cut]
                score_grads = (
                    probs * (dots_buf[slot, head, :, cut] - delta_buf[head, 0:1, cut]) * scale
                ).astype(jnp.bfloat16)
                probs = probs.astype(jnp.bfloat16)
                key_part += contract(qg_buf[head, :, cut], score_grads, 1, 1)
                value_part += contract(qg_buf[HEADS + head, :, cut], probs, 1, 1)
                acc_buf[head, :, cut] += contract(key_t, score_grads, 1, 0)
                acc_buf[HEADS + head, :, cut] += contract(value_t, probs, 1, 0)
            part_buf[head] = key_part
            part_buf[HEADS + head] = value_part

    def pass_on(outgoing, incoming, hop, sems, device, arrived, first, count):
        if arrived is not None:
            arrived.wait_recv()

        @pl.loop(first, first + count)
        def _(index):
            term = part_buf[index]
            if arrived is not None:
                if hop == 1:
                    known = index < HEADS if sems == 0 else index >= HEADS
                    before = incoming[0, index].astype(jnp.float32)
                    term = term + jnp.where(known, before, 0.0)
                else:
                    term = term + incoming[hop - 1, index].astype(jnp.float32)
            outgoing[hop, index] = term.astype(jnp.bfloat16)

        at = pl.ds(first, count)
        return send(
            outgoing.at[hop, at],
            incoming.at[hop, at],
            sum_send.at[sems * half_ring + hop],
            sum_recv.at[sems * half_ring + hop],
            device,
        )

    def clear(ref, first):
        ref[0, pl.ds(first, HEADS)] = jnp.zeros((HEADS, HEAD_DIM, BLOCK), jnp.bfloat16)

    clear(right_in, HEADS)
    clear(left_in, 0)
    grads_of(half_ring)
    to_right = pass_on(right_out, right_in, 0, 0, right, None, 0, HEADS)
    to_left = pass_on(left_out, left_in, 0, 1, left, None, HEADS, HEADS)
    for hop in range(1, half_ring):
        grads_of(half_ring + hop)
        to_right = pass_on(right_out, right_in, hop, 0, right, to_right, 0, 2 * HEADS)
        grads_of(half_ring - hop)
        to_left = pass_on(left_out, left_in, hop, 1, left, to_left, 0, 2 * HEADS)
    grads_of(0)

    @pl.loop(0, 2 * HEADS)
    def _(index):
        core_out[0, index] = acc_buf[index, :, lanes(core_col)].astype(jnp.bfloat16)
        core_out[1, index] = acc_buf[index, :, lanes((core_col + 2) % 4)].astype(jnp.bfloat16)

    far = send(core_out.at[1], core_in.at[1], col_send.at[1], col_recv.at[1], core_peer)
    near = send(core_out.at[0], core_in.at[0], col_send.at[0], col_recv.at[0], core_peer)
    far.wait_recv()

    @pl.loop(0, 2 * HEADS)
    def _(index):
        chip_out[index] = (
            acc_buf[index, :, lanes(chip_col)] + core_in[1, index].astype(jnp.float32)
        ).astype(jnp.bfloat16)

    across = send(chip_out, chip_in, col_send.at[2], col_recv.at[2], chip_peer)
    near.wait_recv()
    to_right.wait_recv()
    to_left.wait_recv()

    @pl.loop(0, HEADS)
    def _(head):
        for first, ref in ((0, kgrad_ref), (HEADS, vgrad_ref)):
            index = head + first
            ref[head] = (
                part_buf[index]
                + right_in[half_ring - 1, index].astype(jnp.float32)
                + left_in[half_ring - 1, index].astype(jnp.float32)
            )

    across.wait_recv()

    @pl.loop(0, HEADS)
    def _(head):
        def summed(index):
            return (
                acc_buf[index, :, lanes(col)]
                + core_in[0, index].astype(jnp.float32)
                + chip_in[index].astype(jnp.float32)
            )

        qgrad_ref[head] = summed(head)
        att_ref[head] = summed(HEADS + head).astype(jnp.bfloat16)

    for copy in pending:
        copy.wait_send()


def fused(n_ring, n_col, queries, key_rows, values, out_grad, block_pairs, pair_count, edge_mask):
    vmem = pl.BlockSpec(memory_space=pltpu.VMEM)
    smem = pl.BlockSpec(memory_space=pltpu.SMEM)
    block = (2 * HEADS, HEAD_DIM, BLOCK)
    wide = n_col * BLOCK
    flat = (HEADS, HEAD_DIM, BLOCK)
    qg_own, kv_own, bias = pl.pallas_call(
        prepare_kernel,
        out_shape=(
            jax.ShapeDtypeStruct(block, jnp.bfloat16),
            jax.ShapeDtypeStruct(block, jnp.bfloat16),
            jax.ShapeDtypeStruct((n_ring, n_col, BLOCK, BLOCK), jnp.float32),
        ),
        in_specs=[smem] * 2 + [vmem] * 5,
        out_specs=(vmem, vmem, vmem),
        compiler_params=pltpu.CompilerParams(vmem_limit_bytes=24 * 2**20),
    )(block_pairs[0], pair_count, queries, key_rows, values, out_grad, edge_mask[0])
    half = n_ring // 2
    dma = pltpu.SemaphoreType.DMA
    outs = pl.pallas_call(
        functools.partial(layer_kernel, n_ring),
        out_shape=(
            jax.ShapeDtypeStruct(flat, jnp.bfloat16),
            jax.ShapeDtypeStruct(flat, jnp.float32),
            jax.ShapeDtypeStruct(flat, jnp.float32),
            jax.ShapeDtypeStruct(flat, jnp.float32),
        ),
        in_specs=[vmem] * 3,
        out_specs=(vmem,) * 4,
        scratch_shapes=[
            pltpu.VMEM((n_ring,) + block, jnp.bfloat16),
            pltpu.VMEM((2 * HEADS, HEAD_DIM, wide), jnp.bfloat16),
            pltpu.VMEM((n_ring, HEADS, BLOCK, wide), jnp.float32),
            pltpu.VMEM((n_ring, HEADS, BLOCK, wide), jnp.float32),
            pltpu.VMEM((n_ring, HEADS, 8, wide), jnp.float32),
            pltpu.VMEM((4, HEADS, 8, wide), jnp.float32),
            pltpu.VMEM((HEADS, n_ring, wide), jnp.float32),
            pltpu.VMEM((HEADS, 8, wide), jnp.float32),
            pltpu.VMEM((2 * HEADS, HEAD_DIM, wide), jnp.float32),
            pltpu.VMEM(block, jnp.float32),
            pltpu.VMEM((half,) + block, jnp.bfloat16),
            pltpu.VMEM((half,) + block, jnp.bfloat16),
            pltpu.VMEM((half,) + block, jnp.bfloat16),
            pltpu.VMEM((half,) + block, jnp.bfloat16),
            pltpu.VMEM((2,) + block, jnp.bfloat16),
            pltpu.VMEM((2,) + block, jnp.bfloat16),
            pltpu.VMEM(block, jnp.bfloat16),
            pltpu.VMEM(block, jnp.bfloat16),
            dma((2 * half + 1,)),
            dma((2 * half + 1,)),
            dma((3,)),
            dma((3,)),
            dma((4,)),
            dma((4,)),
            dma((2 * half,)),
            dma((2 * half,)),
            dma((3,)),
            dma((3,)),
            dma((1,)),
        ],
        compiler_params=pltpu.CompilerParams(
            collective_id=0, has_side_effects=True, vmem_limit_bytes=60 * 2**20
        ),
    )(qg_own, kv_own, bias)
    return tuple(jnp.transpose(out.reshape(HEADS * HEAD_DIM, BLOCK)) for out in outs)


def solution(mesh):
    n_row, n_col = mesh.shape["row"], mesh.shape["col"]
    placed = (
        P(("row", "col"), None),
        P(("col", "row"), None),
        P(("col", "row"), None),
        P(("row", "col"), None),
        P(("row", "col"), None, None),
        P(("row", "col")),
        P(("row", "col"), None, None, None),
    )

    def layer(queries, key_rows, values, out_grad, block_pairs, pair_count, edge_mask):
        args = (queries, key_rows, values, out_grad, block_pairs, pair_count, edge_mask)
        one_block = queries.shape[0] == BLOCK and key_rows.shape[0] == BLOCK
        full_tile = edge_mask.shape[1] == n_row * n_col
        if one_block and full_tile and n_row == 8 and n_col == 4:
            return fused(n_row, n_col, *args)
        return on_device(*args)

    return jax.shard_map(
        layer,
        mesh=mesh,
        in_specs=placed,
        out_specs=(
            P(("row", "col"), None),
            P(("row", "col"), None),
            P(("col", "row"), None),
            P(("col", "row"), None),
        ),
        check_vma=False,
    )
```

```python
import functools

import jax
import jax.numpy as jnp
from jax import lax
from jax.experimental import pallas as pl
from jax.experimental.pallas import tpu as pltpu
from jax.sharding import PartitionSpec as P

HEADS = 8
HEAD_DIM = 96
BLOCK = 128


NEGATIVE = -1e30


def on_device(queries, key_rows, values, out_grad, block_pairs, pair_count, edge_mask):
    score_scale = HEAD_DIM ** (-0.5)
    targets, cotangent = (
        lax.all_gather(queries, "col", axis=0, tiled=True),
        lax.all_gather(out_grad, "col", axis=0, tiled=True),
    )
    sources, source_values = (
        lax.all_gather(key_rows, "row", axis=0, tiled=True),
        lax.all_gather(values, "row", axis=0, tiled=True),
    )
    own_rows = queries.shape[0]
    target_rows = targets.shape[0]
    source_rows = sources.shape[0]
    target_blocks = target_rows // BLOCK
    source_blocks = source_rows // BLOCK
    query_blocks = targets.reshape(target_blocks, BLOCK, HEADS, HEAD_DIM)
    grad_blocks = cotangent.reshape(target_blocks, BLOCK, HEADS, HEAD_DIM)
    key_blocks = sources.reshape(source_blocks, BLOCK, HEADS, HEAD_DIM)
    value_blocks = source_values.reshape(source_blocks, BLOCK, HEADS, HEAD_DIM)
    slot_total = edge_mask.shape[1]
    group_size = min(8, slot_total)
    turn_count = slot_total // group_size
    pair_list = block_pairs[0]
    live_slots = jnp.arange(slot_total, dtype=jnp.int32) < pair_count[0]
    keep_all = (edge_mask[0] > 0) & live_slots[:, None, None]

    def group_scores(turn_index):
        first_slot = turn_index * group_size
        target_ids = lax.dynamic_slice_in_dim(pair_list[:, 0], first_slot, group_size)
        source_ids = lax.dynamic_slice_in_dim(pair_list[:, 1], first_slot, group_size)
        keep_mask = lax.dynamic_slice_in_dim(keep_all, first_slot, group_size, 0)[:, None, :, :]
        scores = (
            jnp.einsum(
                "gihd,gjhd->ghij",
                query_blocks[target_ids],
                key_blocks[source_ids],
                preferred_element_type=jnp.float32,
            )
            * score_scale
        )
        return (target_ids, source_ids, keep_mask, scores)

    def max_turn(turn_index, running_max):
        target_ids, source_ids, keep_mask, scores = group_scores(turn_index)
        row_top = jnp.max(jnp.where(keep_mask, scores, NEGATIVE), axis=3)
        return running_max.at[target_ids].max(row_top)

    local_max = lax.fori_loop(
        0, turn_count, max_turn, jnp.full((target_blocks, HEADS, BLOCK), NEGATIVE, jnp.float32)
    )
    row_max = lax.pmax(local_max, "col")

    def sum_turn(turn_index, carry):
        numer_sum, weight_sum = carry
        target_ids, source_ids, keep_mask, scores = group_scores(turn_index)
        weights = jnp.exp(jnp.where(keep_mask, scores - row_max[target_ids][..., None], NEGATIVE))
        rounded = weights.astype(jnp.bfloat16)
        mixed = jnp.einsum(
            "ghij,gjhd->gihd", rounded, value_blocks[source_ids], preferred_element_type=jnp.float32
        )
        numer_sum = numer_sum.at[target_ids].add(mixed.reshape(group_size, BLOCK, HEADS * HEAD_DIM))
        weight_sum = weight_sum.at[target_ids].add(jnp.sum(weights, axis=3))
        return (numer_sum, weight_sum)

    numer_init = jnp.zeros((target_blocks, BLOCK, HEADS * HEAD_DIM), jnp.float32)
    total_init = jnp.zeros((target_blocks, HEADS, BLOCK), jnp.float32)
    numer_sum, weight_sum = lax.fori_loop(0, turn_count, sum_turn, (numer_init, total_init))
    numer_flat = numer_sum.reshape(target_rows, HEADS * HEAD_DIM)
    numer_all, total_all = lax.psum((numer_flat, weight_sum), "col")
    heads_out = (
        numer_all.reshape(target_blocks, BLOCK, HEADS, HEAD_DIM)
        / jnp.transpose(total_all, (0, 2, 1))[..., None]
    )
    out_all = heads_out.astype(jnp.bfloat16).reshape(target_rows, HEADS * HEAD_DIM)
    attention_out = lax.dynamic_slice_in_dim(out_all, lax.axis_index("col") * own_rows, own_rows, 0)
    products = (cotangent.astype(jnp.float32) * out_all.astype(jnp.float32)).reshape(
        target_blocks, BLOCK, HEADS, HEAD_DIM
    )
    row_delta = jnp.transpose(jnp.sum(products, axis=3), (0, 2, 1))

    def back_turn(turn_index, carry):
        query_acc, key_acc, value_acc = carry
        target_ids, source_ids, keep_mask, scores = group_scores(turn_index)
        probs = (
            jnp.exp(jnp.where(keep_mask, scores - row_max[target_ids][..., None], NEGATIVE))
            / total_all[target_ids][..., None]
        )
        grad_group = grad_blocks[target_ids]
        grad_dots = jnp.einsum(
            "gihd,gjhd->ghij",
            grad_group,
            value_blocks[source_ids],
            preferred_element_type=jnp.float32,
        )
        score_grads = (probs * (grad_dots - row_delta[target_ids][..., None]) * score_scale).astype(
            jnp.bfloat16
        )
        probs_rounded = probs.astype(jnp.bfloat16)
        query_part = jnp.einsum(
            "ghij,gjhd->gihd",
            score_grads,
            key_blocks[source_ids],
            preferred_element_type=jnp.float32,
        )
        key_part = jnp.einsum(
            "ghij,gihd->gjhd",
            score_grads,
            query_blocks[target_ids],
            preferred_element_type=jnp.float32,
        )
        value_part = jnp.einsum(
            "ghij,gihd->gjhd", probs_rounded, grad_group, preferred_element_type=jnp.float32
        )
        query_acc = query_acc.at[target_ids].add(
            query_part.reshape(group_size, BLOCK, HEADS * HEAD_DIM)
        )
        key_acc = key_acc.at[source_ids].add(key_part.reshape(group_size, BLOCK, HEADS * HEAD_DIM))
        value_acc = value_acc.at[source_ids].add(
            value_part.reshape(group_size, BLOCK, HEADS * HEAD_DIM)
        )
        return (query_acc, key_acc, value_acc)

    query_init = jnp.zeros((target_blocks, BLOCK, HEADS * HEAD_DIM), jnp.float32)
    source_init = jnp.zeros((source_blocks, BLOCK, HEADS * HEAD_DIM), jnp.float32)
    query_acc, key_acc, value_acc = lax.fori_loop(
        0, turn_count, back_turn, (query_init, source_init, source_init)
    )
    query_grad = lax.psum_scatter(
        query_acc.reshape(target_rows, HEADS * HEAD_DIM), "col", scatter_dimension=0, tiled=True
    )
    key_grad, value_grad = (
        lax.psum_scatter(
            key_acc.reshape(source_rows, HEADS * HEAD_DIM), "row", scatter_dimension=0, tiled=True
        ),
        lax.psum_scatter(
            value_acc.reshape(source_rows, HEADS * HEAD_DIM), "row", scatter_dimension=0, tiled=True
        ),
    )
    return (attention_out, query_grad, key_grad, value_grad)


MASKED = -1e30
FLOOR = -1e28
MESH = pl.DeviceIdType.MESH


def contract(left, right, left_dim, right_dim):
    return lax.dot_general(
        left,
        right,
        (((left_dim,), (right_dim,)), ((), ())),
        preferred_element_type=jnp.float32,
    )


def write_kernel(*refs):
    count = (len(refs) - 2) // 3
    ins, outs, held = refs[:count], refs[count : 2 * count], refs[2 * count : 3 * count]
    read_sem, write_sem = refs[3 * count :]
    reads = [pltpu.make_async_copy(ins[k], held[k], read_sem.at[k]) for k in range(count)]
    writes = [pltpu.make_async_copy(held[k], outs[k], write_sem.at[k]) for k in range(count)]
    for copy in reads:
        copy.start()
    for k in range(count):
        reads[k].wait()
        writes[k].start()
    for copy in writes:
        copy.wait()


def layer_kernel(
    n_ring,
    pair_ref,
    count_ref,
    q_ref,
    k_ref,
    v_ref,
    g_ref,
    mask_ref,
    att_ref,
    qgrad_ref,
    kgrad_ref,
    vgrad_ref,
    raw_buf,
    mask_buf,
    bias_ref,
    qg_own,
    att_buf,
    grad_bufs,
    kv_buf,
    qg_buf,
    weight_buf,
    dots_buf,
    chunk_stats,
    stat_buf,
    factor_buf,
    delta_buf,
    acc_buf,
    part_buf,
    right_out,
    right_in,
    left_out,
    left_in,
    core_out,
    core_in,
    chip_out,
    chip_in,
    ring_send,
    ring_recv,
    qg_send,
    qg_recv,
    stat_send,
    stat_recv,
    sum_send,
    sum_recv,
    col_send,
    col_recv,
    own_sem,
    load_sem,
    save_sem,
):
    scale = HEAD_DIM ** (-0.5)
    row = lax.axis_index("row")
    col = lax.axis_index("col")
    half_ring = n_ring // 2
    depth, side = row // 2, row % 2
    place = jnp.where(side == 0, depth, n_ring - 1 - depth)

    def row_at(position):
        wrapped = lax.rem(position + 2 * n_ring, n_ring)
        return jnp.where(wrapped < half_ring, 2 * wrapped, 2 * (n_ring - 1 - wrapped) + 1)

    right = (row_at(place + 1), col)
    left = (row_at(place - 1), col)
    core_col = col + 1 - 2 * (col % 2)
    chip_col = (col + 2) % 4
    core_peer = (row, core_col)
    chip_peer = (row, chip_col)
    others = [(row, (col + k) % 4) for k in range(1, 4)]
    pending = []

    def send(src, dst, send_sem, recv_sem, device):
        copy = pltpu.make_async_remote_copy(
            src_ref=src,
            dst_ref=dst,
            send_sem=send_sem,
            recv_sem=recv_sem,
            device_id=device,
            device_id_type=MESH,
        )
        copy.start()
        pending.append(copy)
        return copy

    loads = [
        pltpu.make_async_copy(ref, raw_buf.at[k], load_sem.at[k])
        for k, ref in enumerate((k_ref, v_ref, q_ref, g_ref))
    ]
    loads.append(pltpu.make_async_copy(mask_ref, mask_buf, load_sem.at[4]))
    for load in loads:
        load.start()
    barrier = pltpu.get_barrier_semaphore()
    for device in [right, left] + others:
        pl.semaphore_signal(barrier, inc=1, device_id=device, device_id_type=MESH)

    def turn(index):
        loads[index].wait()
        turned = jnp.transpose(raw_buf[index].astype(jnp.float32)).astype(jnp.bfloat16)
        return turned.reshape(HEADS, HEAD_DIM, BLOCK)

    kv_buf[0, 0:HEADS] = turn(0)
    kv_buf[0, HEADS:] = turn(1)
    pl.semaphore_wait(barrier, 5)

    def lanes(index):
        return pl.ds(pl.multiple_of(index * BLOCK, BLOCK), BLOCK)

    def ring_part(step, way, part):
        first = HEADS * (part ^ way)
        at = pl.ds(first, HEADS)
        at_sem = (2 * (step - 1) + part) * 2 + way
        src = (step - 1, (n_ring - step + 1) % n_ring)[way]
        dst = (step, n_ring - step)[way]
        return send(
            kv_buf.at[src, at],
            kv_buf.at[dst, at],
            ring_send.at[at_sem],
            ring_recv.at[at_sem],
            (right, left)[way],
        )

    coming = [[ring_part(1, way, part) for way in range(2)] for part in range(2)]
    qg_own[0:HEADS] = turn(2)
    qg_own[HEADS:] = turn(3)
    from_chip = send(qg_own, qg_buf.at[:, :, lanes(col)], qg_send.at[0], qg_recv.at[0], chip_peer)
    from_core = send(qg_own, qg_buf.at[:, :, lanes(col)], qg_send.at[1], qg_recv.at[1], core_peer)
    own_copy = pltpu.make_async_copy(qg_own, qg_buf.at[:, :, lanes(col)], own_sem.at[0])
    own_copy.start()
    loads[4].wait()

    @pl.loop(0, bias_ref.shape[0] * bias_ref.shape[1])
    def _(cell):
        source, target = cell // bias_ref.shape[1], cell % bias_ref.shape[1]
        slot, live = jnp.int32(0), jnp.int32(0)
        for t in range(mask_buf.shape[0]):
            hit = (pair_ref[0, t] == target) & (pair_ref[1, t] == source) & (t < count_ref[0])
            slot = jnp.where(hit, t, slot)
            live = jnp.where(hit, 1, live)
        kept = jnp.transpose((mask_buf[slot] * live).astype(jnp.float32))
        bias_ref[source, target] = jnp.where(kept > 0.5, 0.0, MASKED)

    own_copy.wait()
    from_chip.wait_recv()
    passed = send(
        qg_buf.at[:, :, lanes(chip_col)],
        qg_buf.at[:, :, lanes(chip_col)],
        qg_send.at[2],
        qg_recv.at[2],
        core_peer,
    )
    from_core.wait_recv()
    passed.wait_recv()

    width = 2 * BLOCK
    parts = qg_buf.shape[2] // width

    def stats_of(slot):
        source = row_at(place - slot)

        @pl.loop(0, HEADS)
        def _(head):
            key_t = kv_buf[slot, head]
            value_t = kv_buf[slot, HEADS + head]
            for part in range(parts):
                cut = pl.ds(part * width, width)
                bias = jnp.concatenate(
                    [bias_ref[source, 2 * part], bias_ref[source, 2 * part + 1]], axis=1
                )
                scores = contract(key_t, qg_buf[head, :, cut], 0, 0) * scale + bias
                dots = contract(value_t, qg_buf[HEADS + head, :, cut], 0, 0)
                top = jnp.maximum(jnp.max(scores, axis=0, keepdims=True), FLOOR)
                weights = jnp.exp(scores - top)
                weight_buf[slot, head, :, cut] = weights
                dots_buf[slot, head, :, cut] = dots
                chunk_stats[slot, head, 0:1, cut] = top
                chunk_stats[slot, head, 1:2, cut] = jnp.sum(weights, axis=0, keepdims=True)
                chunk_stats[slot, head, 2:3, cut] = jnp.sum(weights * dots, axis=0, keepdims=True)

    ready = [0]
    for step in range(1, half_ring + 1):
        for part in range(2 if step < half_ring else 1):
            for way in range(2):
                coming[part][way].wait_recv()
                if step + 1 < half_ring or (step + 1 == half_ring and part == 0):
                    coming[part][way] = ring_part(step + 1, way, part)
            if ready:
                stats_of(ready.pop(0))
        while ready:
            stats_of(ready.pop(0))
        ready = [step, n_ring - step] if step < half_ring else [step]
    for slot in ready:
        stats_of(slot)

    @pl.loop(0, HEADS)
    def _(head):
        top = chunk_stats[0, head, 0:1]
        for slot in range(1, n_ring):
            top = jnp.maximum(top, chunk_stats[slot, head, 0:1])
        total = jnp.zeros_like(top)
        mixed = jnp.zeros_like(top)
        for slot in range(n_ring):
            factor = jnp.exp(chunk_stats[slot, head, 0:1] - top)
            total = total + factor * chunk_stats[slot, head, 1:2]
            mixed = mixed + factor * chunk_stats[slot, head, 2:3]
        stat_buf[0, head, 0:1] = top
        stat_buf[0, head, 1:2] = total
        stat_buf[0, head, 2:3] = mixed

    shared = [
        send(stat_buf.at[0], stat_buf.at[k], stat_send.at[k], stat_recv.at[k], others[k - 1])
        for k in range(1, 4)
    ]
    acc_buf[...] = jnp.zeros(acc_buf.shape, jnp.float32)
    for copy in shared:
        copy.wait_recv()

    @pl.loop(0, HEADS)
    def _(head):
        top = stat_buf[0, head, 0:1]
        for k in range(1, 4):
            top = jnp.maximum(top, stat_buf[k, head, 0:1])
        total = jnp.zeros_like(top)
        mixed = jnp.zeros_like(top)
        for k in range(4):
            factor = jnp.exp(stat_buf[k, head, 0:1] - top)
            total = total + factor * stat_buf[k, head, 1:2]
            mixed = mixed + factor * stat_buf[k, head, 2:3]
        inverse = 1.0 / total
        delta_buf[head, 0:1] = mixed * inverse
        for slot in range(n_ring):
            factor_buf[head, slot : slot + 1] = (
                jnp.exp(chunk_stats[slot, head, 0:1] - top) * inverse
            )

    def grads_of(slot, held):
        @pl.loop(0, HEADS)
        def _(head):
            key_t = kv_buf[slot, head]
            value_t = kv_buf[slot, HEADS + head]
            key_part = jnp.zeros((HEAD_DIM, BLOCK), jnp.float32)
            value_part = jnp.zeros((HEAD_DIM, BLOCK), jnp.float32)
            for part in range(parts):
                cut = pl.ds(part * width, width)
                probs = weight_buf[slot, head, :, cut] * factor_buf[head, slot : slot + 1, cut]
                score_grads = (
                    probs * (dots_buf[slot, head, :, cut] - delta_buf[head, 0:1, cut]) * scale
                ).astype(jnp.bfloat16)
                probs = probs.astype(jnp.bfloat16)
                key_part += contract(qg_buf[head, :, cut], score_grads, 1, 1)
                value_part += contract(qg_buf[HEADS + head, :, cut], probs, 1, 1)
                acc_buf[head, :, cut] += contract(key_t, score_grads, 1, 0)
                acc_buf[HEADS + head, :, cut] += contract(value_t, probs, 1, 0)
            part_buf[held, head] = key_part
            part_buf[held, HEADS + head] = value_part

    sums = {}

    def pass_on(hop, way, part, held):
        outgoing = (right_out, left_out)[way]
        incoming = (right_in, left_in)[way]
        first = HEADS * (part ^ way)
        arrived = sums.get((hop - 1, way, part))
        if arrived is not None:
            arrived.wait_recv()

        @pl.loop(first, first + HEADS)
        def _(index):
            term = part_buf[held, index]
            if arrived is not None:
                term = term + incoming[hop - 1, index].astype(jnp.float32)
            outgoing[hop, index] = term.astype(jnp.bfloat16)

        at = pl.ds(first, HEADS)
        at_sem = (2 * hop + part) * 2 + way
        sums[hop, way, part] = send(
            outgoing.at[hop, at],
            incoming.at[hop, at],
            sum_send.at[at_sem],
            sum_recv.at[at_sem],
            (right, left)[way],
        )

    last = half_ring - 1
    grads_of(half_ring, 0)
    pass_on(0, 0, 0, 0)
    pass_on(0, 1, 0, 0)
    grads_of(half_ring + 1, 2)
    grads_of(half_ring - 1, 3)
    for hop in range(1, last):
        now, later = 2 * (hop % 2), 2 * ((hop + 1) % 2)
        pass_on(hop, 0, 0, now)
        pass_on(hop, 1, 0, now + 1)
        grads_of(half_ring + hop + 1, later)
        pass_on(hop, 0, 1, now)
        pass_on(hop, 1, 1, now + 1)
        grads_of(half_ring - hop - 1, later + 1)
    now, own = 2 * (last % 2), 2 * ((last + 1) % 2)
    pass_on(last, 0, 0, now)
    pass_on(last, 1, 0, now + 1)
    grads_of(0, own)

    @pl.loop(0, 2 * HEADS)
    def _(index):
        core_out[0, index] = acc_buf[index, :, lanes(core_col)].astype(jnp.bfloat16)
        core_out[1, index] = acc_buf[index, :, lanes((core_col + 2) % 4)].astype(jnp.bfloat16)

    far = send(core_out.at[1], core_in.at[1], col_send.at[1], col_recv.at[1], core_peer)
    near = send(core_out.at[0], core_in.at[0], col_send.at[0], col_recv.at[0], core_peer)
    pass_on(last, 0, 1, now)
    pass_on(last, 1, 1, now + 1)
    far.wait_recv()

    @pl.loop(0, 2 * HEADS)
    def _(index):
        chip_out[index] = (
            acc_buf[index, :, lanes(chip_col)] + core_in[1, index].astype(jnp.float32)
        ).astype(jnp.bfloat16)

    across = send(chip_out, chip_in, col_send.at[2], col_recv.at[2], chip_peer)
    near.wait_recv()

    def summed(first):
        at = pl.ds(first, HEADS)
        return (
            acc_buf[at, :, lanes(col)]
            + core_in[0, at].astype(jnp.float32)
            + chip_in[at].astype(jnp.float32)
        )

    def natural(value):
        return jnp.transpose(value.reshape(HEADS * HEAD_DIM, BLOCK))

    saves = []

    def save(src, dst):
        copy = pltpu.make_async_copy(src, dst, save_sem.at[len(saves)])
        copy.start()
        saves.append(copy)

    for way in range(2):
        for part in range(2):
            sums[last, way, part].wait_recv()
    for k, ref in ((0, kgrad_ref), (1, vgrad_ref)):
        at = pl.ds(k * HEADS, HEADS)
        grad_bufs[k] = natural(
            part_buf[own, at]
            + right_in[half_ring - 1, at].astype(jnp.float32)
            + left_in[half_ring - 1, at].astype(jnp.float32)
        )
        save(grad_bufs.at[k], ref)

    across.wait_recv()
    grad_bufs[2] = natural(summed(0))
    save(grad_bufs.at[2], qgrad_ref)
    att_buf[...] = natural(summed(HEADS)).astype(jnp.bfloat16)
    save(att_buf, att_ref)
    for copy in saves:
        copy.wait()
    for copy in pending:
        copy.wait_send()


def fused(n_ring, n_col, queries, key_rows, values, out_grad, block_pairs, pair_count, edge_mask):
    smem = pl.BlockSpec(memory_space=pltpu.SMEM)
    placed = pl.BlockSpec(memory_space=pl.ANY)
    block = (2 * HEADS, HEAD_DIM, BLOCK)
    wide = n_col * BLOCK
    rows, features = queries.shape
    slots = edge_mask.shape[1]
    half = n_ring // 2
    dma = pltpu.SemaphoreType.DMA
    shapes = tuple(
        jax.ShapeDtypeStruct((rows, features), kind)
        for kind in (jnp.bfloat16, jnp.float32, jnp.float32, jnp.float32)
    )
    outs = pl.pallas_call(
        functools.partial(layer_kernel, n_ring),
        out_shape=shapes,
        in_specs=[smem] * 2 + [placed] * 5,
        out_specs=(placed,) * 4,
        scratch_shapes=[
            pltpu.VMEM((4, rows, features), jnp.bfloat16),
            pltpu.VMEM((slots, BLOCK, BLOCK), jnp.int32),
            pltpu.VMEM((n_ring, n_col, BLOCK, BLOCK), jnp.float32),
            pltpu.VMEM(block, jnp.bfloat16),
            pltpu.VMEM((rows, features), jnp.bfloat16),
            pltpu.VMEM((3, rows, features), jnp.float32),
            pltpu.VMEM((n_ring,) + block, jnp.bfloat16),
            pltpu.VMEM((2 * HEADS, HEAD_DIM, wide), jnp.bfloat16),
            pltpu.VMEM((n_ring, HEADS, BLOCK, wide), jnp.float32),
            pltpu.VMEM((n_ring, HEADS, BLOCK, wide), jnp.float32),
            pltpu.VMEM((n_ring, HEADS, 8, wide), jnp.float32),
            pltpu.VMEM((4, HEADS, 8, wide), jnp.float32),
            pltpu.VMEM((HEADS, n_ring, wide), jnp.float32),
            pltpu.VMEM((HEADS, 8, wide), jnp.float32),
            pltpu.VMEM((2 * HEADS, HEAD_DIM, wide), jnp.float32),
            pltpu.VMEM((4,) + block, jnp.float32),
            pltpu.VMEM((half,) + block, jnp.bfloat16),
            pltpu.VMEM((half,) + block, jnp.bfloat16),
            pltpu.VMEM((half,) + block, jnp.bfloat16),
            pltpu.VMEM((half,) + block, jnp.bfloat16),
            pltpu.VMEM((2,) + block, jnp.bfloat16),
            pltpu.VMEM((2,) + block, jnp.bfloat16),
            pltpu.VMEM(block, jnp.bfloat16),
            pltpu.VMEM(block, jnp.bfloat16),
            dma((4 * half,)),
            dma((4 * half,)),
            dma((3,)),
            dma((3,)),
            dma((4,)),
            dma((4,)),
            dma((4 * half,)),
            dma((4 * half,)),
            dma((3,)),
            dma((3,)),
            dma((1,)),
            dma((5,)),
            dma((4,)),
        ],
        compiler_params=pltpu.CompilerParams(
            collective_id=0, has_side_effects=True, vmem_limit_bytes=61 * 2**20
        ),
    )(jnp.transpose(block_pairs[0]), pair_count, queries, key_rows, values, out_grad, edge_mask[0])
    return pl.pallas_call(
        write_kernel,
        out_shape=shapes,
        in_specs=[placed] * 4,
        out_specs=(placed,) * 4,
        scratch_shapes=[pltpu.VMEM(shape.shape, shape.dtype) for shape in shapes]
        + [dma((4,)), dma((4,))],
        compiler_params=pltpu.CompilerParams(vmem_limit_bytes=61 * 2**20),
    )(*outs)


def solution(mesh):
    n_row, n_col = mesh.shape["row"], mesh.shape["col"]
    placed = (
        P(("row", "col"), None),
        P(("col", "row"), None),
        P(("col", "row"), None),
        P(("row", "col"), None),
        P(("row", "col"), None, None),
        P(("row", "col")),
        P(("row", "col"), None, None, None),
    )

    def layer(queries, key_rows, values, out_grad, block_pairs, pair_count, edge_mask):
        args = (queries, key_rows, values, out_grad, block_pairs, pair_count, edge_mask)
        one_block = queries.shape[0] == BLOCK and key_rows.shape[0] == BLOCK
        full_tile = edge_mask.shape[1] == n_row * n_col
        if one_block and full_tile and n_row == 8 and n_col == 4:
            return fused(n_row, n_col, *args)
        return on_device(*args)

    return jax.shard_map(
        layer,
        mesh=mesh,
        in_specs=placed,
        out_specs=(
            P(("row", "col"), None),
            P(("row", "col"), None),
            P(("col", "row"), None),
            P(("col", "row"), None),
        ),
        check_vma=False,
    )
```

```python
import functools

import jax
import jax.numpy as jnp
from jax import lax
from jax.experimental import pallas as pl
from jax.experimental.pallas import tpu as pltpu
from jax.sharding import PartitionSpec as P

HEADS = 8
HEAD_DIM = 96
BLOCK = 128


NEGATIVE = -1e30


def on_device(queries, key_rows, values, out_grad, block_pairs, pair_count, edge_mask):
    score_scale = HEAD_DIM ** (-0.5)
    targets, cotangent = (
        lax.all_gather(queries, "col", axis=0, tiled=True),
        lax.all_gather(out_grad, "col", axis=0, tiled=True),
    )
    sources, source_values = (
        lax.all_gather(key_rows, "row", axis=0, tiled=True),
        lax.all_gather(values, "row", axis=0, tiled=True),
    )
    own_rows = queries.shape[0]
    target_rows = targets.shape[0]
    source_rows = sources.shape[0]
    target_blocks = target_rows // BLOCK
    source_blocks = source_rows // BLOCK
    query_blocks = targets.reshape(target_blocks, BLOCK, HEADS, HEAD_DIM)
    grad_blocks = cotangent.reshape(target_blocks, BLOCK, HEADS, HEAD_DIM)
    key_blocks = sources.reshape(source_blocks, BLOCK, HEADS, HEAD_DIM)
    value_blocks = source_values.reshape(source_blocks, BLOCK, HEADS, HEAD_DIM)
    slot_total = edge_mask.shape[1]
    group_size = min(8, slot_total)
    turn_count = slot_total // group_size
    pair_list = block_pairs[0]
    live_slots = jnp.arange(slot_total, dtype=jnp.int32) < pair_count[0]
    keep_all = (edge_mask[0] > 0) & live_slots[:, None, None]

    def group_scores(turn_index):
        first_slot = turn_index * group_size
        target_ids = lax.dynamic_slice_in_dim(pair_list[:, 0], first_slot, group_size)
        source_ids = lax.dynamic_slice_in_dim(pair_list[:, 1], first_slot, group_size)
        keep_mask = lax.dynamic_slice_in_dim(keep_all, first_slot, group_size, 0)[:, None, :, :]
        scores = (
            jnp.einsum(
                "gihd,gjhd->ghij",
                query_blocks[target_ids],
                key_blocks[source_ids],
                preferred_element_type=jnp.float32,
            )
            * score_scale
        )
        return (target_ids, source_ids, keep_mask, scores)

    def max_turn(turn_index, running_max):
        target_ids, source_ids, keep_mask, scores = group_scores(turn_index)
        row_top = jnp.max(jnp.where(keep_mask, scores, NEGATIVE), axis=3)
        return running_max.at[target_ids].max(row_top)

    local_max = lax.fori_loop(
        0, turn_count, max_turn, jnp.full((target_blocks, HEADS, BLOCK), NEGATIVE, jnp.float32)
    )
    row_max = lax.pmax(local_max, "col")

    def sum_turn(turn_index, carry):
        numer_sum, weight_sum = carry
        target_ids, source_ids, keep_mask, scores = group_scores(turn_index)
        weights = jnp.exp(jnp.where(keep_mask, scores - row_max[target_ids][..., None], NEGATIVE))
        rounded = weights.astype(jnp.bfloat16)
        mixed = jnp.einsum(
            "ghij,gjhd->gihd", rounded, value_blocks[source_ids], preferred_element_type=jnp.float32
        )
        numer_sum = numer_sum.at[target_ids].add(mixed.reshape(group_size, BLOCK, HEADS * HEAD_DIM))
        weight_sum = weight_sum.at[target_ids].add(jnp.sum(weights, axis=3))
        return (numer_sum, weight_sum)

    numer_init = jnp.zeros((target_blocks, BLOCK, HEADS * HEAD_DIM), jnp.float32)
    total_init = jnp.zeros((target_blocks, HEADS, BLOCK), jnp.float32)
    numer_sum, weight_sum = lax.fori_loop(0, turn_count, sum_turn, (numer_init, total_init))
    numer_flat = numer_sum.reshape(target_rows, HEADS * HEAD_DIM)
    numer_all, total_all = lax.psum((numer_flat, weight_sum), "col")
    heads_out = (
        numer_all.reshape(target_blocks, BLOCK, HEADS, HEAD_DIM)
        / jnp.transpose(total_all, (0, 2, 1))[..., None]
    )
    out_all = heads_out.astype(jnp.bfloat16).reshape(target_rows, HEADS * HEAD_DIM)
    attention_out = lax.dynamic_slice_in_dim(out_all, lax.axis_index("col") * own_rows, own_rows, 0)
    products = (cotangent.astype(jnp.float32) * out_all.astype(jnp.float32)).reshape(
        target_blocks, BLOCK, HEADS, HEAD_DIM
    )
    row_delta = jnp.transpose(jnp.sum(products, axis=3), (0, 2, 1))

    def back_turn(turn_index, carry):
        query_acc, key_acc, value_acc = carry
        target_ids, source_ids, keep_mask, scores = group_scores(turn_index)
        probs = (
            jnp.exp(jnp.where(keep_mask, scores - row_max[target_ids][..., None], NEGATIVE))
            / total_all[target_ids][..., None]
        )
        grad_group = grad_blocks[target_ids]
        grad_dots = jnp.einsum(
            "gihd,gjhd->ghij",
            grad_group,
            value_blocks[source_ids],
            preferred_element_type=jnp.float32,
        )
        score_grads = (probs * (grad_dots - row_delta[target_ids][..., None]) * score_scale).astype(
            jnp.bfloat16
        )
        probs_rounded = probs.astype(jnp.bfloat16)
        query_part = jnp.einsum(
            "ghij,gjhd->gihd",
            score_grads,
            key_blocks[source_ids],
            preferred_element_type=jnp.float32,
        )
        key_part = jnp.einsum(
            "ghij,gihd->gjhd",
            score_grads,
            query_blocks[target_ids],
            preferred_element_type=jnp.float32,
        )
        value_part = jnp.einsum(
            "ghij,gihd->gjhd", probs_rounded, grad_group, preferred_element_type=jnp.float32
        )
        query_acc = query_acc.at[target_ids].add(
            query_part.reshape(group_size, BLOCK, HEADS * HEAD_DIM)
        )
        key_acc = key_acc.at[source_ids].add(key_part.reshape(group_size, BLOCK, HEADS * HEAD_DIM))
        value_acc = value_acc.at[source_ids].add(
            value_part.reshape(group_size, BLOCK, HEADS * HEAD_DIM)
        )
        return (query_acc, key_acc, value_acc)

    query_init = jnp.zeros((target_blocks, BLOCK, HEADS * HEAD_DIM), jnp.float32)
    source_init = jnp.zeros((source_blocks, BLOCK, HEADS * HEAD_DIM), jnp.float32)
    query_acc, key_acc, value_acc = lax.fori_loop(
        0, turn_count, back_turn, (query_init, source_init, source_init)
    )
    query_grad = lax.psum_scatter(
        query_acc.reshape(target_rows, HEADS * HEAD_DIM), "col", scatter_dimension=0, tiled=True
    )
    key_grad, value_grad = (
        lax.psum_scatter(
            key_acc.reshape(source_rows, HEADS * HEAD_DIM), "row", scatter_dimension=0, tiled=True
        ),
        lax.psum_scatter(
            value_acc.reshape(source_rows, HEADS * HEAD_DIM), "row", scatter_dimension=0, tiled=True
        ),
    )
    return (attention_out, query_grad, key_grad, value_grad)


MASKED = -1e30
FLOOR = -1e28
MESH = pl.DeviceIdType.MESH
PIECES = 4
LOG2_E = 1.4426950408889634


def contract(left, right, left_dim, right_dim):
    return lax.dot_general(
        left,
        right,
        (((left_dim,), (right_dim,)), ((), ())),
        preferred_element_type=jnp.float32,
    )


def write_kernel(*refs):
    count = (len(refs) - 2) // 3
    ins, outs, held = refs[:count], refs[count : 2 * count], refs[2 * count : 3 * count]
    read_sem, write_sem = refs[3 * count :]
    reads = [pltpu.make_async_copy(ins[k], held[k], read_sem.at[k]) for k in range(count)]
    writes = [pltpu.make_async_copy(held[k], outs[k], write_sem.at[k]) for k in range(count)]
    for copy in reads:
        copy.start()
    for k in range(count):
        reads[k].wait()
        writes[k].start()
    for copy in writes:
        copy.wait()


def layer_kernel(
    n_ring,
    pair_ref,
    count_ref,
    q_ref,
    k_ref,
    v_ref,
    g_ref,
    mask_ref,
    att_ref,
    qgrad_ref,
    kgrad_ref,
    vgrad_ref,
    raw_buf,
    mask_buf,
    bias_ref,
    qg_own,
    att_buf,
    grad_bufs,
    kv_buf,
    qg_buf,
    weight_buf,
    dots_buf,
    chunk_stats,
    stat_buf,
    factor_buf,
    delta_buf,
    acc_buf,
    part_buf,
    right_out,
    right_in,
    left_out,
    left_in,
    core_out,
    core_in,
    chip_out,
    chip_in,
    ring_send,
    ring_recv,
    qg_send,
    qg_recv,
    stat_send,
    stat_recv,
    sum_send,
    sum_recv,
    col_send,
    col_recv,
    own_sem,
    load_sem,
    save_sem,
):
    scale = HEAD_DIM ** (-0.5)
    group = 2 * HEADS // PIECES
    row = lax.axis_index("row")
    col = lax.axis_index("col")
    half_ring = n_ring // 2
    depth, side = row // 2, row % 2
    place = jnp.where(side == 0, depth, n_ring - 1 - depth)

    def row_at(position):
        wrapped = lax.rem(position + 2 * n_ring, n_ring)
        return jnp.where(wrapped < half_ring, 2 * wrapped, 2 * (n_ring - 1 - wrapped) + 1)

    right = (row_at(place + 1), col)
    left = (row_at(place - 1), col)
    core_col = col + 1 - 2 * (col % 2)
    chip_col = (col + 2) % 4
    core_peer = (row, core_col)
    chip_peer = (row, chip_col)
    others = [(row, (col + k) % 4) for k in range(1, 4)]
    pending = []

    def send(src, dst, send_sem, recv_sem, device):
        copy = pltpu.make_async_remote_copy(
            src_ref=src,
            dst_ref=dst,
            send_sem=send_sem,
            recv_sem=recv_sem,
            device_id=device,
            device_id_type=MESH,
        )
        copy.start()
        pending.append(copy)
        return copy

    loads = [
        pltpu.make_async_copy(ref, raw_buf.at[k], load_sem.at[k])
        for k, ref in enumerate((k_ref, v_ref, q_ref, g_ref))
    ]
    loads.append(pltpu.make_async_copy(mask_ref, mask_buf, load_sem.at[4]))
    for load in loads:
        load.start()
    barrier = pltpu.get_barrier_semaphore()
    for device in [right, left] + others:
        pl.semaphore_signal(barrier, inc=1, device_id=device, device_id_type=MESH)

    def turn(index):
        loads[index].wait()
        turned = jnp.transpose(raw_buf[index].astype(jnp.float32)).astype(jnp.bfloat16)
        return turned.reshape(HEADS, HEAD_DIM, BLOCK)

    kv_buf[0, 0:HEADS] = turn(0)
    kv_buf[0, HEADS:] = turn(1)
    pl.semaphore_wait(barrier, 5)

    def lanes(index):
        return pl.ds(pl.multiple_of(index * BLOCK, BLOCK), BLOCK)

    def ring_part(step, way, part):
        at = pl.ds((group * part + HEADS * way) % (2 * HEADS), group)
        at_sem = (PIECES * (step - 1) + part) * 2 + way
        src = (step - 1, (n_ring - step + 1) % n_ring)[way]
        dst = (step, n_ring - step)[way]
        return send(
            kv_buf.at[src, at],
            kv_buf.at[dst, at],
            ring_send.at[at_sem],
            ring_recv.at[at_sem],
            (right, left)[way],
        )

    coming = [[ring_part(1, way, part) for way in range(2)] for part in range(PIECES)]
    qg_own[0:HEADS] = turn(2)
    qg_own[HEADS:] = turn(3)
    from_chip = send(qg_own, qg_buf.at[:, :, lanes(col)], qg_send.at[0], qg_recv.at[0], chip_peer)
    from_core = send(qg_own, qg_buf.at[:, :, lanes(col)], qg_send.at[1], qg_recv.at[1], core_peer)
    own_copy = pltpu.make_async_copy(qg_own, qg_buf.at[:, :, lanes(col)], own_sem.at[0])
    own_copy.start()
    loads[4].wait()

    @pl.loop(0, bias_ref.shape[0] * bias_ref.shape[1])
    def _(cell):
        source, target = cell // bias_ref.shape[1], cell % bias_ref.shape[1]
        slot, live = jnp.int32(0), jnp.int32(0)
        for t in range(mask_buf.shape[0]):
            hit = (pair_ref[0, t] == target) & (pair_ref[1, t] == source) & (t < count_ref[0])
            slot = jnp.where(hit, t, slot)
            live = jnp.where(hit, 1, live)
        kept = jnp.transpose((mask_buf[slot] * live).astype(jnp.float32))
        bias_ref[source, target] = jnp.where(kept > 0.5, 0.0, MASKED)

    own_copy.wait()
    from_chip.wait_recv()
    passed = send(
        qg_buf.at[:, :, lanes(chip_col)],
        qg_buf.at[:, :, lanes(chip_col)],
        qg_send.at[2],
        qg_recv.at[2],
        core_peer,
    )
    from_core.wait_recv()
    passed.wait_recv()

    width = 2 * BLOCK
    parts = qg_buf.shape[2] // width

    def stats_of(slot, piece):
        source = row_at(place - slot)
        few = HEADS // PIECES * 2

        @pl.loop(piece * few, piece * few + few, unroll=2)
        def _(head):
            key_t = kv_buf[slot, head]
            value_t = kv_buf[slot, HEADS + head]
            for part in range(parts):
                cut = pl.ds(part * width, width)
                bias = jnp.concatenate(
                    [bias_ref[source, 2 * part], bias_ref[source, 2 * part + 1]], axis=1
                )
                scores = contract(key_t, qg_buf[head, :, cut], 0, 0) * (scale * LOG2_E) + bias
                dots = contract(value_t, qg_buf[HEADS + head, :, cut], 0, 0)
                top = jnp.maximum(jnp.max(scores, axis=0, keepdims=True), FLOOR)
                weights = jnp.exp2(scores - top)
                weight_buf[slot, head, :, cut] = weights
                dots_buf[slot, head, :, cut] = dots
                at = pl.ds(head, 1)
                chunk_stats[slot, 0, at, cut] = top
                chunk_stats[slot, 1, at, cut] = jnp.sum(weights, axis=0, keepdims=True)
                chunk_stats[slot, 2, at, cut] = jnp.sum(weights * dots, axis=0, keepdims=True)

    work = PIECES // 2
    ready = [(0, piece) for piece in range(work)]
    for step in range(1, half_ring + 1):
        pieces = PIECES if step < half_ring else PIECES // 2
        for part in range(pieces):
            for way in range(2):
                coming[part][way].wait_recv()
                if step + 1 < half_ring or (step + 1 == half_ring and part < PIECES // 2):
                    coming[part][way] = ring_part(step + 1, way, part)
            if ready:
                stats_of(*ready.pop(0))
        while ready:
            stats_of(*ready.pop(0))
        slots = [step, n_ring - step] if step < half_ring else [step]
        ready = [(slot, piece) for slot in slots for piece in range(work)]
    for item in ready:
        stats_of(*item)

    top = chunk_stats[0, 0]
    for slot in range(1, n_ring):
        top = jnp.maximum(top, chunk_stats[slot, 0])
    total = jnp.zeros_like(top)
    mixed = jnp.zeros_like(top)
    for slot in range(n_ring):
        factor = jnp.exp2(chunk_stats[slot, 0] - top)
        total = total + factor * chunk_stats[slot, 1]
        mixed = mixed + factor * chunk_stats[slot, 2]
    stat_buf[0, 0] = top
    stat_buf[0, 1] = total
    stat_buf[0, 2] = mixed

    shared = [
        send(stat_buf.at[0], stat_buf.at[k], stat_send.at[k], stat_recv.at[k], others[k - 1])
        for k in range(1, 4)
    ]
    acc_buf[...] = jnp.zeros(acc_buf.shape, jnp.float32)
    for copy in shared:
        copy.wait_recv()

    top = stat_buf[0, 0]
    for k in range(1, 4):
        top = jnp.maximum(top, stat_buf[k, 0])
    total = jnp.zeros_like(top)
    mixed = jnp.zeros_like(top)
    for k in range(4):
        factor = jnp.exp2(stat_buf[k, 0] - top)
        total = total + factor * stat_buf[k, 1]
        mixed = mixed + factor * stat_buf[k, 2]
    inverse = 1.0 / total
    delta_buf[...] = mixed * inverse
    for slot in range(n_ring):
        factor_buf[slot] = jnp.exp2(chunk_stats[slot, 0] - top) * inverse

    def grads_of(slot, held, piece):
        few = HEADS // PIECES * 2

        @pl.loop(piece * few, piece * few + few, unroll=2)
        def _(head):
            key_t = kv_buf[slot, head]
            value_t = kv_buf[slot, HEADS + head]
            key_part = jnp.zeros((HEAD_DIM, BLOCK), jnp.float32)
            value_part = jnp.zeros((HEAD_DIM, BLOCK), jnp.float32)
            for part in range(parts):
                cut = pl.ds(part * width, width)
                probs = weight_buf[slot, head, :, cut] * factor_buf[slot, pl.ds(head, 1), cut]
                score_grads = (
                    probs * (dots_buf[slot, head, :, cut] - delta_buf[pl.ds(head, 1), cut]) * scale
                ).astype(jnp.bfloat16)
                probs = probs.astype(jnp.bfloat16)
                key_part += contract(qg_buf[head, :, cut], score_grads, 1, 1)
                value_part += contract(qg_buf[HEADS + head, :, cut], probs, 1, 1)
                acc_buf[head, :, cut] += contract(key_t, score_grads, 1, 0)
                acc_buf[HEADS + head, :, cut] += contract(value_t, probs, 1, 0)
            part_buf[held, head] = key_part
            part_buf[held, HEADS + head] = value_part

    sums = {}

    def pass_on(hop, way, part, held):
        outgoing = (right_out, left_out)[way]
        incoming = (right_in, left_in)[way]
        first = (group * part + HEADS * way) % (2 * HEADS)
        arrived = sums.get((hop - 1, way, part))
        if arrived is not None:
            arrived.wait_recv()

        @pl.loop(first, first + group)
        def _(index):
            term = part_buf[held, index]
            if arrived is not None:
                term = term + incoming[hop - 1, index].astype(jnp.float32)
            outgoing[hop, index] = term.astype(jnp.bfloat16)

        at = pl.ds(first, group)
        at_sem = (PIECES * hop + part) * 2 + way
        sums[hop, way, part] = send(
            outgoing.at[hop, at],
            incoming.at[hop, at],
            sum_send.at[at_sem],
            sum_recv.at[at_sem],
            (right, left)[way],
        )

    last = half_ring - 1
    for piece in range(work):
        grads_of(half_ring, 0, piece)
        pass_on(0, 0, piece, 0)
        pass_on(0, 1, piece, 0)
    for piece in range(work):
        grads_of(half_ring + 1, 2, piece)
        grads_of(half_ring - 1, 3, piece)
    for hop in range(1, last):
        now, later = 2 * (hop % 2), 2 * ((hop + 1) % 2)
        todo = [
            (slot, held, piece)
            for piece in range(work)
            for slot, held in (
                (half_ring + hop + 1, later),
                (half_ring - hop - 1, later + 1),
            )
        ]
        for part in range(PIECES):
            pass_on(hop, 0, part, now)
            pass_on(hop, 1, part, now + 1)
            if todo:
                grads_of(*todo.pop(0))
        for item in todo:
            grads_of(*item)
    now, own = 2 * (last % 2), 2 * ((last + 1) % 2)
    for part in range(PIECES // 2):
        pass_on(last, 0, part, now)
        pass_on(last, 1, part, now + 1)
        for piece in range(work):
            if piece * (PIECES // 2) // work == part:
                grads_of(0, own, piece)

    @pl.loop(0, 2 * HEADS)
    def _(index):
        core_out[0, index] = acc_buf[index, :, lanes(core_col)].astype(jnp.bfloat16)
        core_out[1, index] = acc_buf[index, :, lanes((core_col + 2) % 4)].astype(jnp.bfloat16)

    far = send(core_out.at[1], core_in.at[1], col_send.at[1], col_recv.at[1], core_peer)
    near = send(core_out.at[0], core_in.at[0], col_send.at[0], col_recv.at[0], core_peer)
    for part in range(PIECES // 2, PIECES):
        pass_on(last, 0, part, now)
        pass_on(last, 1, part, now + 1)
    far.wait_recv()

    @pl.loop(0, 2 * HEADS)
    def _(index):
        chip_out[index] = (
            acc_buf[index, :, lanes(chip_col)] + core_in[1, index].astype(jnp.float32)
        ).astype(jnp.bfloat16)

    across = send(chip_out, chip_in, col_send.at[2], col_recv.at[2], chip_peer)
    near.wait_recv()

    def summed(first):
        at = pl.ds(first, HEADS)
        return (
            acc_buf[at, :, lanes(col)]
            + core_in[0, at].astype(jnp.float32)
            + chip_in[at].astype(jnp.float32)
        )

    def natural(value):
        return jnp.transpose(value.reshape(HEADS * HEAD_DIM, BLOCK))

    saves = []

    def save(src, dst):
        copy = pltpu.make_async_copy(src, dst, save_sem.at[len(saves)])
        copy.start()
        saves.append(copy)

    for way in range(2):
        for part in range(PIECES):
            sums[last, way, part].wait_recv()
    for k, ref in ((0, kgrad_ref), (1, vgrad_ref)):
        at = pl.ds(k * HEADS, HEADS)
        grad_bufs[k] = natural(
            part_buf[own, at]
            + right_in[half_ring - 1, at].astype(jnp.float32)
            + left_in[half_ring - 1, at].astype(jnp.float32)
        )
        save(grad_bufs.at[k], ref)

    across.wait_recv()
    grad_bufs[2] = natural(summed(0))
    save(grad_bufs.at[2], qgrad_ref)
    att_buf[...] = natural(summed(HEADS)).astype(jnp.bfloat16)
    save(att_buf, att_ref)
    for copy in saves:
        copy.wait()
    for copy in pending:
        copy.wait_send()


def fused(n_ring, n_col, queries, key_rows, values, out_grad, block_pairs, pair_count, edge_mask):
    smem = pl.BlockSpec(memory_space=pltpu.SMEM)
    placed = pl.BlockSpec(memory_space=pl.ANY)
    block = (2 * HEADS, HEAD_DIM, BLOCK)
    wide = n_col * BLOCK
    rows, features = queries.shape
    slots = edge_mask.shape[1]
    half = n_ring // 2
    dma = pltpu.SemaphoreType.DMA
    shapes = tuple(
        jax.ShapeDtypeStruct((rows, features), kind)
        for kind in (jnp.bfloat16, jnp.float32, jnp.float32, jnp.float32)
    )
    outs = pl.pallas_call(
        functools.partial(layer_kernel, n_ring),
        out_shape=shapes,
        in_specs=[smem] * 2 + [placed] * 5,
        out_specs=(placed,) * 4,
        scratch_shapes=[
            pltpu.VMEM((4, rows, features), jnp.bfloat16),
            pltpu.VMEM((slots, BLOCK, BLOCK), jnp.int32),
            pltpu.VMEM((n_ring, n_col, BLOCK, BLOCK), jnp.float32),
            pltpu.VMEM(block, jnp.bfloat16),
            pltpu.VMEM((rows, features), jnp.bfloat16),
            pltpu.VMEM((3, rows, features), jnp.float32),
            pltpu.VMEM((n_ring,) + block, jnp.bfloat16),
            pltpu.VMEM((2 * HEADS, HEAD_DIM, wide), jnp.bfloat16),
            pltpu.VMEM((n_ring, HEADS, BLOCK, wide), jnp.float32),
            pltpu.VMEM((n_ring, HEADS, BLOCK, wide), jnp.float32),
            pltpu.VMEM((n_ring, 3, HEADS, wide), jnp.float32),
            pltpu.VMEM((4, 3, HEADS, wide), jnp.float32),
            pltpu.VMEM((n_ring, HEADS, wide), jnp.float32),
            pltpu.VMEM((HEADS, wide), jnp.float32),
            pltpu.VMEM((2 * HEADS, HEAD_DIM, wide), jnp.float32),
            pltpu.VMEM((4,) + block, jnp.float32),
            pltpu.VMEM((half,) + block, jnp.bfloat16),
            pltpu.VMEM((half,) + block, jnp.bfloat16),
            pltpu.VMEM((half,) + block, jnp.bfloat16),
            pltpu.VMEM((half,) + block, jnp.bfloat16),
            pltpu.VMEM((2,) + block, jnp.bfloat16),
            pltpu.VMEM((2,) + block, jnp.bfloat16),
            pltpu.VMEM(block, jnp.bfloat16),
            pltpu.VMEM(block, jnp.bfloat16),
            dma((2 * PIECES * half,)),
            dma((2 * PIECES * half,)),
            dma((3,)),
            dma((3,)),
            dma((4,)),
            dma((4,)),
            dma((2 * PIECES * half,)),
            dma((2 * PIECES * half,)),
            dma((3,)),
            dma((3,)),
            dma((1,)),
            dma((5,)),
            dma((4,)),
        ],
        compiler_params=pltpu.CompilerParams(
            collective_id=0, has_side_effects=True, vmem_limit_bytes=61 * 2**20
        ),
    )(jnp.transpose(block_pairs[0]), pair_count, queries, key_rows, values, out_grad, edge_mask[0])
    return pl.pallas_call(
        write_kernel,
        out_shape=shapes,
        in_specs=[placed] * 4,
        out_specs=(placed,) * 4,
        scratch_shapes=[pltpu.VMEM(shape.shape, shape.dtype) for shape in shapes]
        + [dma((4,)), dma((4,))],
        compiler_params=pltpu.CompilerParams(vmem_limit_bytes=61 * 2**20),
    )(*outs)


def solution(mesh):
    n_row, n_col = mesh.shape["row"], mesh.shape["col"]
    placed = (
        P(("row", "col"), None),
        P(("col", "row"), None),
        P(("col", "row"), None),
        P(("row", "col"), None),
        P(("row", "col"), None, None),
        P(("row", "col")),
        P(("row", "col"), None, None, None),
    )

    def layer(queries, key_rows, values, out_grad, block_pairs, pair_count, edge_mask):
        args = (queries, key_rows, values, out_grad, block_pairs, pair_count, edge_mask)
        one_block = queries.shape[0] == BLOCK and key_rows.shape[0] == BLOCK
        full_tile = edge_mask.shape[1] == n_row * n_col
        if one_block and full_tile and n_row == 8 and n_col == 4:
            return fused(n_row, n_col, *args)
        return on_device(*args)

    return jax.shard_map(
        layer,
        mesh=mesh,
        in_specs=placed,
        out_specs=(
            P(("row", "col"), None),
            P(("row", "col"), None),
            P(("col", "row"), None),
            P(("col", "row"), None),
        ),
        check_vma=False,
    )
```
